32 devices in a mesh: groups: 2 (over y), dp: 4 (over z), expert: 4 (over x, core).
Axes of the slice: x: 2, y: 2, z: 4, core: 2. Of those that a mesh axis runs over, the one named last changes fastest.
Arguments:
- tokens: bfloat16 [4096, 4096], P(('groups', 'dp', 'expert')), parts along dimension 0, may hold values from -6 to 6
- assign: int32 [4096, 8], P(('groups', 'dp', 'expert')), parts along dimension 0, may hold values from 0 to 127, all different within a row
- probs: float32 [4096, 8], P(('groups', 'dp', 'expert')), parts along dimension 0, may hold values from 0.1 to 1
- expert_weights: bfloat16 [4, 3, 768, 4096], P('dp', None, 'expert'), may hold values from -4 to 4
Outputs:
- mixed: bfloat16 [4096, 4096], P(('groups', 'dp', 'expert')), parts along dimension 0
The draws below stay inside these ranges and needn't reach their ends.
There are 2 independent parts, one for each index of `groups`. The reference program is written for one: setup_inputs(seed, part) draws one part's arguments, and reference() takes and returns one part's arrays. A program takes and returns all parts, laid end to end along the dimension named above; an argument that names none is the same for every part. Nothing has to cross between parts.
All inputs are finite; a program needn't handle non-finite values.
Results may differ from the reference program's by a relative error of at most 0.0058.
Values may be sent and summed in bfloat16 or wider, within the bound.
No kernel may reach another device: no remote copies, remote signals or barrier semaphores. Data moves between devices by JAX's collectives and lax.ppermute only.
A program may use at most 128 MiB of HBM per device.

```python
import math
import jax
import jax.numpy as jnp
from jax import lax

D = 4096
TOP = 8
ROUTED = 128
FF = 768
TOK_DEV = 128
CAP = 16
EXP_WIN = 4
TOKENS = 2048
N_DP = 4
N_EXPERT = 4


def draw_expert_weights(key, part):
    key = jax.random.fold_in(key, 11)
    shape = (EXP_WIN, 3, FF, D)
    base = jax.random.truncated_normal(key, -4.0, 4.0, shape, jnp.float32)
    scales = jnp.array([D ** (-0.5), D ** (-0.5), FF ** (-0.5)], jnp.float32)
    return (base * scales[None, :, None, None]).astype(jnp.bfloat16)


def levels(key, dims, cuts, least, top_value):
    level = 1.0
    for dim, parts in cuts:
        heights = jax.random.uniform(jax.random.fold_in(jax.random.fold_in(key, 6), dim), (parts,), jnp.float32, least / len(cuts), top_value / len(cuts))
        level = level * jnp.repeat(jnp.exp(heights), dims[dim] // parts).reshape((-1,) + (1,) * (len(dims) - 1 - dim))
    return level


def picks_of(stream_key, rows, count, top, lift):
    sequence = jax.random.permutation(jax.random.fold_in(stream_key, 1), count)
    boost = sequence
    for power in range(3):
        boost = boost * boost // count
    boost = boost * lift // count
    lots = jax.random.randint(jax.random.fold_in(stream_key, 2), (rows, count), 0, 4096) + boost
    sure = jax.random.permutation(jax.random.fold_in(stream_key, 3), rows)[jnp.arange(count) % rows]
    lots = jnp.where(jnp.arange(rows)[:, None] == sure[None, :], 1 << 14, lots)
    score = lots * count + jnp.arange(count)
    return lax.top_k(score.astype(jnp.int32), top)[1].astype(jnp.int32)


def normal_values(rng, extent, scale, most, shards=(), kind=jnp.bfloat16):
    loudness = levels(rng, extent, shards, -0.22, 0.18) if shards else 1.0
    values = jax.random.normal(rng, extent, jnp.float32) * scale * loudness
    return jnp.minimum(jnp.maximum(values, -most), most).astype(kind)


def setup_inputs(seed: int = 0, part: int = 0) -> dict:
    key_of = jax.random.split(jax.random.key(seed), 5)
    own_keys = jax.random.split(jax.random.fold_in(key_of[4], part), 5)
    return {
        "tokens": normal_values(own_keys[0], (TOKENS, D), 1.0, 6.0, ((0, 16),)),
        "assign": picks_of(own_keys[1], TOKENS, ROUTED, TOP, 1024),
        "probs": jnp.clip(jnp.exp(math.log(1.0) - 2.3025851 * jax.random.uniform(own_keys[2], (TOKENS, TOP), jnp.float32) ** levels(own_keys[2], (TOKENS, TOP), ((0, 16),), -0.2, 0.2)), 0.1, 1.0),
        "expert_weights": draw_expert_weights(jax.random.fold_in(key_of[4], 71), part),
    }


def routing_slots(assign_block, experts_here, capacity):
    copies = assign_block.shape[0] * assign_block.shape[1]
    flat_ids = assign_block.reshape(copies).astype(jnp.int32)
    labels = jnp.arange(experts_here, dtype=jnp.int32)
    onehot_table = (flat_ids[:, None] == labels[None, :]).astype(jnp.int32)
    earlier = (jnp.cumsum(onehot_table, axis=0, dtype=jnp.int32) - onehot_table).astype(jnp.int32)
    position = jnp.sum(earlier * onehot_table, axis=1, dtype=jnp.int32)
    inside = jnp.sum(onehot_table, axis=1, dtype=jnp.int32)
    kept_mask = (inside > 0) & (position < capacity)
    dump_slot = experts_here * capacity
    slot_of = jnp.where(kept_mask, flat_ids * capacity + position, dump_slot).astype(jnp.int32)
    owner_token = (jnp.arange(copies, dtype=jnp.int32) // assign_block.shape[1]).astype(jnp.int32)
    slot_token = jnp.zeros((dump_slot + 1,), jnp.int32).at[slot_of].set(owner_token)[:dump_slot]
    filled = jnp.zeros((dump_slot + 1,), jnp.int32).at[slot_of].set(jnp.ones_like(owner_token))[:dump_slot]
    return slot_of.reshape(assign_block.shape), kept_mask.reshape(assign_block.shape), slot_token, filled


def dispatch_rows(tok_rows, slot_token, filled):
    picked = jnp.take(tok_rows, slot_token, axis=0)
    return jnp.where(filled[:, None] > 0, picked, jnp.zeros_like(picked))


def combine_copies(returned, slot_of, kept_mask, weights):
    limit = returned.shape[0] - 1
    total = jnp.zeros((slot_of.shape[0], returned.shape[1]), jnp.float32)
    for rank in range(slot_of.shape[1]):
        picked = jnp.take(returned, jnp.minimum(slot_of[:, rank], limit), axis=0).astype(jnp.float32)
        factor = jnp.where(kept_mask[:, rank], weights[:, rank], jnp.zeros_like(weights[:, rank]))
        total = total + factor[:, None] * picked
    return total.astype(jnp.bfloat16)


def expert_apply(rows_in, slab):
    both = jnp.einsum("rd,kfd->krf", rows_in.astype(jnp.float32), slab[:2].astype(jnp.float32))
    hidden = (jax.nn.silu(both[0]) * both[1]).astype(jnp.bfloat16)
    return jnp.dot(hidden, slab[2], preferred_element_type=jnp.float32)


def reference(tokens, assign, probs, expert_weights):
    blocks = N_DP * N_EXPERT
    tok_blocks = tokens.reshape(blocks, TOK_DEV, D)
    assign_blocks = assign.reshape(blocks, TOK_DEV, TOP)
    prob_blocks = probs.reshape(blocks, TOK_DEV, TOP)

    def tables(block):
        return routing_slots(block, EXP_WIN, CAP)

    slot_of, kept_mask, slot_token, filled = jax.vmap(tables)(assign_blocks)
    sent = jax.vmap(dispatch_rows)(tok_blocks, slot_token, filled)
    by_expert = sent.reshape(blocks, EXP_WIN, CAP, D).transpose(1, 0, 2, 3).reshape(EXP_WIN, blocks * CAP, D)

    def one_expert(pair):
        return expert_apply(pair[0], pair[1]).astype(jnp.bfloat16)

    outputs = lax.map(one_expert, (by_expert, expert_weights))
    returned = outputs.reshape(EXP_WIN, blocks, CAP, D).transpose(1, 0, 2, 3).reshape(blocks, EXP_WIN * CAP, D)

    def one_block(group):
        return combine_copies(group[0], group[1], group[2], group[3])

    mixed = lax.map(one_block, (returned, slot_of, kept_mask, prob_blocks))
    return mixed.reshape(blocks * TOK_DEV, D)
```

```python
import functools
import jax
import jax.numpy as jnp
from jax import lax
from jax.experimental import pallas as pl
from jax.experimental.pallas import tpu as pltpu
from jax.sharding import PartitionSpec as P

NT = (((1,), (1,)), ((), ()))
WHOLE = pl.BlockSpec(memory_space=pltpu.VMEM)
ANYWHERE = pl.BlockSpec(memory_space=pl.ANY)


def swap(block, axis, mask):
    route = [(i ^ mask, i) for i in range(lax.axis_size(axis))]
    return lax.ppermute(block, axis, route)


def dispatch_kernel(experts, cap, assign_ref, probs_ref, tok_ref, *outs):
    rows_out, mix_out = outs[:-1], outs[-1]
    top, toks = assign_ref.shape
    slots = experts * cap
    me = lax.axis_index("dp")
    place = lax.broadcasted_iota(jnp.int32, (slots, toks), 0)
    label = (place // cap) ^ me
    hit = jnp.zeros((slots, toks), jnp.float32)
    weight = jnp.zeros((slots, toks), jnp.float32)
    for k in range(top):
        same = assign_ref[k : k + 1, :] == label
        hit = hit + same.astype(jnp.float32)
        weight = weight + jnp.where(same, probs_ref[k : k + 1, :], 0.0)
    first = lax.broadcasted_iota(jnp.int32, (toks, toks), 0)
    second = lax.broadcasted_iota(jnp.int32, (toks, toks), 1)
    earlier = (first < second).astype(jnp.bfloat16)
    position = jnp.dot(
        hit.astype(jnp.bfloat16), earlier, preferred_element_type=jnp.float32
    )
    here = (hit > 0.0) & (position == (place % cap).astype(jnp.float32))
    pick = here.astype(jnp.bfloat16)
    for m in range(experts):
        rows_out[m][...] = jnp.dot(
            pick[m * cap : (m + 1) * cap],
            tok_ref[...],
            preferred_element_type=jnp.float32,
        ).astype(jnp.bfloat16)
    factor = jnp.where(here, weight, 0.0).T
    high = factor.astype(jnp.bfloat16)
    rest = factor - high.astype(jnp.float32)
    middle = rest.astype(jnp.bfloat16)
    low = (rest - middle.astype(jnp.float32)).astype(jnp.bfloat16)
    mix_out[...] = jnp.concatenate([high, middle, low], axis=1)


def dispatch(assign, probs, tokens, experts, cap):
    toks, width = tokens.shape
    return pl.pallas_call(
        functools.partial(dispatch_kernel, experts, cap),
        out_shape=[jax.ShapeDtypeStruct((cap, width), jnp.bfloat16)] * experts
        + [jax.ShapeDtypeStruct((toks, 3 * experts * cap), jnp.bfloat16)],
        in_specs=[WHOLE] * 3,
        out_specs=[WHOLE] * (experts + 1),
        name="dispatch",
    )(assign.T, probs.T, tokens)


def expert_kernel(count, steps, *refs):
    slabs, blocks, outs = refs[:2], refs[2 : 2 + count], refs[2 + count : 2 + 2 * count]
    rows, enter, leave, sems = refs[2 + 2 * count :]
    units, width = slabs[0].shape[1:]
    cap = blocks[0].shape[0]
    span = width // steps

    def fetch(phase, step, j):
        cols = pl.ds(step * span, span)
        if phase == 0:
            return pltpu.make_async_copy(
                slabs[j].at[0:2, :, cols], enter.at[2 * j : 2 * j + 2, :, cols], sems.at[phase, step, j]
            )
        return pltpu.make_async_copy(
            slabs[j].at[2, :, cols], leave.at[j, :, cols], sems.at[phase, step, j]
        )

    for phase in range(2):
        for step in range(steps):
            for j in range(2):
                fetch(phase, step, j).start()
    for b in range(count):
        rows[b * cap : (b + 1) * cap, :] = blocks[b][...]
    both = jnp.zeros((count * cap, 4 * units), jnp.float32)
    for step in range(steps):
        for j in range(2):
            fetch(0, step, j).wait()
        cols = slice(step * span, (step + 1) * span)
        both = both + lax.dot_general(
            rows[:, cols],
            enter[:, :, cols].reshape(4 * units, span),
            NT,
            preferred_element_type=jnp.float32,
        )
    hidden = []
    for j in range(2):
        gate = both[:, 2 * j * units : (2 * j + 1) * units]
        up = both[:, (2 * j + 1) * units : (2 * j + 2) * units]
        hidden.append((jax.nn.silu(gate) * up).astype(jnp.bfloat16))
    hidden = jnp.concatenate(hidden, axis=1)
    for step in range(steps):
        for j in range(2):
            fetch(1, step, j).wait()
        cols = slice(step * span, (step + 1) * span)
        part = jnp.dot(
            hidden,
            leave[:, :, cols].reshape(2 * units, span),
            preferred_element_type=jnp.float32,
        )
        for b in range(count):
            outs[b][:, cols] = part[b * cap : (b + 1) * cap].astype(outs[b].dtype)


def expert_part(own, sibling, blocks, kinds, steps=4):
    count = len(blocks)
    cap, width = blocks[0].shape
    units = own.shape[1]
    return pl.pallas_call(
        functools.partial(expert_kernel, count, steps),
        out_shape=[jax.ShapeDtypeStruct((cap, width), kind) for kind in kinds],
        in_specs=[ANYWHERE] * 2 + [WHOLE] * count,
        out_specs=[WHOLE] * count,
        scratch_shapes=[
            pltpu.VMEM((count * cap, width), jnp.bfloat16),
            pltpu.VMEM((4, units, width), jnp.bfloat16),
            pltpu.VMEM((2, units, width), jnp.bfloat16),
            pltpu.SemaphoreType.DMA((2, steps, 2)),
        ],
        compiler_params=pltpu.CompilerParams(vmem_limit_bytes=48 * 1024 * 1024),
        name="experts",
    )(own, sibling, *blocks)


def combine_kernel(count, mix_ref, *refs):
    rows = jnp.concatenate([ref[...] for ref in refs[:count]], axis=0)
    refs[count][...] = jnp.dot(
        mix_ref[...],
        jnp.concatenate([rows] * 3, axis=0),
        preferred_element_type=jnp.float32,
    ).astype(jnp.bfloat16)


def combine(mix, returned, steps=4):
    count = len(returned)
    cap, width = returned[0].shape
    toks = mix.shape[0]
    span = width // steps
    return pl.pallas_call(
        functools.partial(combine_kernel, count),
        grid=(steps,),
        out_shape=jax.ShapeDtypeStruct((toks, width), jnp.bfloat16),
        in_specs=[pl.BlockSpec(mix.shape, lambda i: (0, 0))]
        + [pl.BlockSpec((cap, span), lambda i: (0, i))] * count,
        out_specs=pl.BlockSpec((toks, span), lambda i: (0, i)),
        name="combine",
    )(mix, *returned)


def local(tokens, assign, probs, expert_weights):
    experts = lax.axis_size("dp")
    chips = lax.axis_size("expert") // 2
    cap = tokens.shape[0] // 8
    own = expert_weights[0]
    sibling = swap(own, "expert", 1)
    *outgoing, mix = dispatch(assign, probs, tokens, experts, cap)
    arrived = [swap(p, "dp", m) if m else p for m, p in enumerate(outgoing)]
    blocks = [
        swap(p, "expert", 2 * c) if c else p for p in arrived for c in range(chips)
    ]
    kinds = [jnp.bfloat16 if c else jnp.float32 for _ in arrived for c in range(chips)]
    parts = expert_part(own, sibling, blocks, kinds)
    returned = []
    for m in range(experts):
        total = parts[m * chips]
        for c in range(1, chips):
            total = total + swap(parts[m * chips + c], "expert", 2 * c).astype(jnp.float32)
        total = total.astype(jnp.bfloat16)
        returned.append(swap(total, "dp", m) if m else total)
    return combine(mix, returned)


def solution(mesh):
    placed = (
        P(("groups", "dp", "expert"), None),
        P(("groups", "dp", "expert"), None),
        P(("groups", "dp", "expert"), None),
        P("dp", None, "expert", None),
    )
    return jax.shard_map(
        local,
        mesh=mesh,
        in_specs=placed,
        out_specs=P(("groups", "dp", "expert"), None),
        check_vma=False,
    )
```

```python
import functools
import jax
import jax.numpy as jnp
from jax import lax
from jax.experimental import pallas as pl
from jax.experimental.pallas import tpu as pltpu
from jax.sharding import PartitionSpec as P

NT = (((1,), (1,)), ((), ()))
WHOLE = pl.BlockSpec(memory_space=pltpu.VMEM)
ANYWHERE = pl.BlockSpec(memory_space=pl.ANY)
MAIN = pl.BlockSpec(memory_space=pltpu.HBM)


def swap(block, axis, mask):
    route = [(i ^ mask, i) for i in range(lax.axis_size(axis))]
    return lax.ppermute(block, axis, route)


def cost(micros):
    return pl.CostEstimate(flops=0, bytes_accessed=int(micros * 3690e3 * 1), transcendentals=0)


def in_main(x):
    return pltpu.with_memory_space_constraint(x, pltpu.HBM)


def slot_table(labels, cap, assign, probs):
    top, toks = assign.shape
    slots = len(labels) * cap
    place = lax.broadcasted_iota(jnp.int32, (slots, toks), 0)
    label = jnp.zeros((slots, toks), jnp.int32)
    for n, expert in enumerate(labels):
        label = jnp.where(place // cap == n, expert, label)
    hit = jnp.zeros((slots, toks), jnp.float32)
    weight = jnp.zeros((slots, toks), jnp.float32)
    for k in range(top):
        same = assign[k : k + 1, :] == label
        hit = jnp.where(same, 1.0, hit)
        if probs is not None:
            weight = jnp.where(same, probs[k : k + 1, :], weight)
    first = lax.broadcasted_iota(jnp.int32, (toks, toks), 0)
    second = lax.broadcasted_iota(jnp.int32, (toks, toks), 1)
    position = jnp.dot(
        hit.astype(jnp.bfloat16),
        (first < second).astype(jnp.bfloat16),
        preferred_element_type=jnp.float32,
    )
    here = (hit > 0.0) & (position == (place % cap).astype(jnp.float32))
    return here, weight


def dispatch_kernel(masks, cap, steps, assign_ref, tok_ref, after_ref, *refs):
    outs, (table, held, sems) = refs[: len(masks)], refs[len(masks) :]
    span = held.shape[1] // steps
    columns = [slice(s * span, (s + 1) * span) for s in range(steps)]
    small = pltpu.make_async_copy(assign_ref, table, sems.at[steps])
    small.start()
    copies = [
        pltpu.make_async_copy(tok_ref.at[:, c], held.at[:, c], sems.at[s])
        for s, c in enumerate(columns)
    ]
    for copy in copies:
        copy.start()
    small.wait()
    me = lax.axis_index("dp")
    here, _ = slot_table([me ^ m for m in masks], cap, table[...], None)
    pick = here.astype(jnp.bfloat16)
    for copy, c in zip(copies, columns):
        copy.wait()
        rows = jnp.dot(pick, held[:, c], preferred_element_type=jnp.float32)
        rows = rows.astype(jnp.bfloat16)
        for n in range(len(masks)):
            outs[n][:, c] = rows[n * cap : (n + 1) * cap]


def dispatch(assign, tokens, masks, cap, after, steps=4):
    toks, width = tokens.shape
    return pl.pallas_call(
        functools.partial(dispatch_kernel, masks, cap, steps),
        out_shape=[jax.ShapeDtypeStruct((cap, width), jnp.bfloat16)] * len(masks),
        in_specs=[MAIN, MAIN, ANYWHERE],
        out_specs=[WHOLE] * len(masks),
        scratch_shapes=[
            pltpu.VMEM(assign.shape[::-1], assign.dtype),
            pltpu.VMEM((toks, width), jnp.bfloat16),
            pltpu.SemaphoreType.DMA((steps + 1,)),
        ],
        compiler_params=pltpu.CompilerParams(vmem_limit_bytes=12 * 1024 * 1024),
        cost_estimate=cost(1.0),
        name="dispatch",
    )(in_main(assign.T), in_main(tokens), after)


def prepare_kernel(
    masks, cap, assign_ref, probs_ref, slab_ref, after_ref, mix_ref, held_ref, ids, gains, sems
):
    copies = [
        pltpu.make_async_copy(assign_ref, ids, sems.at[0]),
        pltpu.make_async_copy(probs_ref, gains, sems.at[1]),
        pltpu.make_async_copy(slab_ref, held_ref, sems.at[2]),
    ]
    for copy in copies:
        copy.start()
    copies[0].wait()
    copies[1].wait()
    me = lax.axis_index("dp")
    here, weight = slot_table([me ^ m for m in masks], cap, ids[...], gains[...])
    factor = jnp.where(here, weight, 0.0).T
    high = factor.astype(jnp.bfloat16)
    rest = factor - high.astype(jnp.float32)
    middle = rest.astype(jnp.bfloat16)
    low = (rest - middle.astype(jnp.float32)).astype(jnp.bfloat16)
    mix_ref[...] = jnp.concatenate([high, middle, low], axis=1)
    copies[2].wait()


def prepare(assign, probs, slab, masks, cap, after):
    toks = assign.shape[0]
    return pl.pallas_call(
        functools.partial(prepare_kernel, masks, cap),
        out_shape=[
            jax.ShapeDtypeStruct((toks, 3 * len(masks) * cap), jnp.bfloat16),
            jax.ShapeDtypeStruct(slab.shape, slab.dtype),
        ],
        in_specs=[MAIN] * 3 + [ANYWHERE],
        out_specs=[WHOLE] * 2,
        scratch_shapes=[
            pltpu.VMEM(assign.shape[::-1], assign.dtype),
            pltpu.VMEM(probs.shape[::-1], probs.dtype),
            pltpu.SemaphoreType.DMA((3,)),
        ],
        compiler_params=pltpu.CompilerParams(vmem_limit_bytes=16 * 1024 * 1024),
        cost_estimate=cost(2.5),
        name="prepare",
    )(in_main(assign.T), in_main(probs.T), in_main(slab), after)


def expert_kernel(count, steps, *refs):
    slabs, blocks, outs, rows = refs[:2], refs[2 : 2 + count], refs[2 + count : -1], refs[-1]
    units, width = slabs[0].shape[1:]
    cap = blocks[0].shape[0]
    span = width // steps
    columns = [slice(s * span, (s + 1) * span) for s in range(steps)]
    for b in range(count):
        rows[b * cap : (b + 1) * cap, :] = blocks[b][...]
    hidden = []
    for slab in slabs:
        both = jnp.zeros((2 * units, count * cap), jnp.float32)
        for c in columns:
            both = both + lax.dot_general(
                slab[0:2, :, c].reshape(2 * units, span),
                rows[:, c],
                NT,
                preferred_element_type=jnp.float32,
            )
        hidden.append((jax.nn.silu(both[:units]) * both[units:]).astype(jnp.bfloat16))
    hidden = jnp.concatenate(hidden, axis=0).T
    for c in columns:
        down = jnp.concatenate([slab[2, :, c] for slab in slabs], axis=0)
        part = jnp.dot(hidden, down, preferred_element_type=jnp.float32)
        start = 0
        for out in outs:
            stop = start + out.shape[0]
            out[:, c] = part[start:stop].astype(out.dtype)
            start = stop


def expert_part(own, sibling, groups, chips, blocks, steps=8):
    keys = [(m, c) for group in groups for c in range(chips) for m in group]
    cap, width = blocks[keys[0]].shape
    shapes = [
        jax.ShapeDtypeStruct((len(group) * cap, width), jnp.bfloat16 if c else jnp.float32)
        for group in groups
        for c in range(chips)
    ]
    parts = pl.pallas_call(
        functools.partial(expert_kernel, len(keys), steps),
        out_shape=shapes,
        in_specs=[WHOLE] * (2 + len(keys)),
        out_specs=[WHOLE] * len(shapes),
        scratch_shapes=[pltpu.VMEM((len(keys) * cap, width), jnp.bfloat16)],
        compiler_params=pltpu.CompilerParams(
            vmem_limit_bytes=(12 + len(keys)) * 1024 * 1024
        ),
        cost_estimate=cost(2.5),
        name="experts",
    )(own, sibling, *[blocks[k] for k in keys])
    return [parts[i * chips : (i + 1) * chips] for i in range(len(groups))]


def combine_kernel(count, steps, mix_ref, *refs):
    blocks, (out_ref, held, sems) = refs[:count], refs[count:]
    span = held.shape[1] // steps
    copies = []
    for s in range(steps):
        c = slice(s * span, (s + 1) * span)
        rows = jnp.concatenate([ref[:, c] for ref in blocks] * 3, axis=0)
        held[:, c] = jnp.dot(
            mix_ref[...], rows, preferred_element_type=jnp.float32
        ).astype(jnp.bfloat16)
        copies.append(pltpu.make_async_copy(held.at[:, c], out_ref.at[:, c], sems.at[s]))
        copies[-1].start()
    for copy in copies:
        copy.wait()


def combine(mix, returned, steps=4):
    count = len(returned)
    cap, width = returned[0].shape
    toks = mix.shape[0]
    return pl.pallas_call(
        functools.partial(combine_kernel, count, steps),
        out_shape=jax.ShapeDtypeStruct((toks, width), jnp.bfloat16),
        in_specs=[WHOLE] * (1 + count),
        out_specs=ANYWHERE,
        scratch_shapes=[
            pltpu.VMEM((toks, width), jnp.bfloat16),
            pltpu.SemaphoreType.DMA((steps,)),
        ],
        compiler_params=pltpu.CompilerParams(vmem_limit_bytes=12 * 1024 * 1024),
        cost_estimate=cost(1.2),
        name="combine",
    )(mix, *returned)


def after(x, *others):
    return lax.optimization_barrier((x, *others))[0]


def total(parts, *others):
    result = parts[0]
    for c in range(1, len(parts)):
        part = after(parts[c], *others) if others else parts[c]
        result = result + swap(part, "expert", 2 * c).astype(jnp.float32)
    return result.astype(jnp.bfloat16)


def local(tokens, assign, probs, expert_weights):
    experts = lax.axis_size("dp")
    chips = lax.axis_size("expert") // 2
    cap = tokens.shape[0] // 8
    own = expert_weights[0]
    near, far = list(range(1, experts // 2)), list(range(experts // 2, experts))
    soon, late = far[: len(far) // 2], far[len(far) // 2 :]
    order = [*soon, *late, *near, 0]
    blocks = {}

    def across(m, *others):
        for c in range(1, chips):
            blocks[m, c] = swap(after(blocks[m, 0], *others), "expert", 2 * c)

    outgoing = dict(zip(order, dispatch(assign, tokens, order, cap, tokens)))
    blocks[0, 0] = outgoing[0]
    across(0)
    for m in soon + near:
        blocks[m, 0] = swap(outgoing[m], "dp", m)
    for m in late:
        blocks[m, 0] = swap(outgoing[m], "dp", m)
    sibling = swap(after(own, outgoing[0]), "expert", 1)
    mix, own = prepare(assign, probs, own, order, cap, outgoing[0])
    for m in soon:
        across(m, mix)
    for m in near:
        across(m)
    for m in late:
        across(m)
    first, second, rest, home = expert_part(own, sibling, [soon, late, near, [0]], chips, blocks)
    results = [(soon, first, ()), (late, second, ()), (near, rest, ()), ([0], home, ())]
    returned, came = {}, {}
    for group, parts, others in results:
        rows = total(parts, *(came.get(o, o) if isinstance(o, int) else o for o in others))
        came[group[-1]] = rows
        for n, m in enumerate(group):
            row = rows[n * cap : (n + 1) * cap]
            returned[m] = swap(row, "dp", m) if m else row
    return combine(mix, [returned[m] for m in order])


def solution(mesh):
    placed = (
        P(("groups", "dp", "expert"), None),
        P(("groups", "dp", "expert"), None),
        P(("groups", "dp", "expert"), None),
        P("dp", None, "expert", None),
    )
    return jax.shard_map(
        local,
        mesh=mesh,
        in_specs=placed,
        out_specs=P(("groups", "dp", "expert"), None),
        check_vma=False,
    )
```

```python
import functools
import jax
import jax.numpy as jnp
from jax import lax
from jax.experimental import pallas as pl
from jax.experimental.pallas import tpu as pltpu
from jax.sharding import PartitionSpec as P

NT = (((1,), (1,)), ((), ()))
WHOLE = pl.BlockSpec(memory_space=pltpu.VMEM)
ANYWHERE = pl.BlockSpec(memory_space=pl.ANY)
MAIN = pl.BlockSpec(memory_space=pltpu.HBM)


def swap(block, axis, mask):
    route = [(i ^ mask, i) for i in range(lax.axis_size(axis))]
    return lax.ppermute(block, axis, route)


def cost(micros):
    return pl.CostEstimate(flops=0, bytes_accessed=int(micros * 3690e3), transcendentals=0)


def in_main(x):
    return pltpu.with_memory_space_constraint(x, pltpu.HBM)


def slot_table(labels, cap, assign, probs):
    top, toks = assign.shape
    slots = len(labels) * cap
    place = lax.broadcasted_iota(jnp.int32, (slots, toks), 0)
    label = jnp.zeros((slots, toks), jnp.int32)
    for n, expert in enumerate(labels):
        label = jnp.where(place // cap == n, expert, label)
    hit = jnp.zeros((slots, toks), jnp.float32)
    weight = jnp.zeros((slots, toks), jnp.float32)
    for k in range(top):
        same = assign[k : k + 1, :] == label
        hit = jnp.where(same, 1.0, hit)
        if probs is not None:
            weight = jnp.where(same, probs[k : k + 1, :], weight)
    first = lax.broadcasted_iota(jnp.int32, (toks, toks), 0)
    second = lax.broadcasted_iota(jnp.int32, (toks, toks), 1)
    position = jnp.dot(
        hit.astype(jnp.bfloat16),
        (first < second).astype(jnp.bfloat16),
        preferred_element_type=jnp.float32,
    )
    here = (hit > 0.0) & (position == (place % cap).astype(jnp.float32))
    return here, weight


def dispatch_kernel(masks, cap, steps, assign_ref, tok_ref, *refs):
    outs, (table, held, sems) = refs[: len(masks)], refs[len(masks) :]
    span = held.shape[1] // steps
    columns = [slice(s * span, (s + 1) * span) for s in range(steps)]
    small = pltpu.make_async_copy(assign_ref, table, sems.at[steps])
    small.start()
    copies = [
        pltpu.make_async_copy(tok_ref.at[:, c], held.at[:, c], sems.at[s])
        for s, c in enumerate(columns)
    ]
    for copy in copies:
        copy.start()
    small.wait()
    me = lax.axis_index("dp")
    here, _ = slot_table([me ^ m for m in masks], cap, table[...], None)
    pick = here.astype(jnp.bfloat16)
    for copy, c in zip(copies, columns):
        copy.wait()
        rows = jnp.dot(pick, held[:, c], preferred_element_type=jnp.float32)
        rows = rows.astype(jnp.bfloat16)
        for n in range(len(masks)):
            outs[n][:, c] = rows[n * cap : (n + 1) * cap]


def dispatch(assign, tokens, masks, cap, steps=2):
    toks, width = tokens.shape
    return pl.pallas_call(
        functools.partial(dispatch_kernel, masks, cap, steps),
        out_shape=[jax.ShapeDtypeStruct((cap, width), jnp.bfloat16)] * len(masks),
        in_specs=[MAIN, MAIN],
        out_specs=[WHOLE] * len(masks),
        scratch_shapes=[
            pltpu.VMEM(assign.shape[::-1], assign.dtype),
            pltpu.VMEM((toks, width), jnp.bfloat16),
            pltpu.SemaphoreType.DMA((steps + 1,)),
        ],
        compiler_params=pltpu.CompilerParams(vmem_limit_bytes=12 * 1024 * 1024),
        cost_estimate=cost(1.0),
        name="dispatch",
    )(in_main(assign.T), in_main(tokens))


def prepare_kernel(
    masks, cap, assign_ref, probs_ref, slab_ref, after_ref, mix_ref, held_ref, ids, gains, sems
):
    copies = [
        pltpu.make_async_copy(assign_ref, ids, sems.at[0]),
        pltpu.make_async_copy(probs_ref, gains, sems.at[1]),
        pltpu.make_async_copy(slab_ref, held_ref, sems.at[2]),
    ]
    for copy in copies:
        copy.start()
    copies[0].wait()
    copies[1].wait()
    me = lax.axis_index("dp")
    here, weight = slot_table([me ^ m for m in masks], cap, ids[...], gains[...])
    factor = jnp.where(here, weight, 0.0).T
    high = factor.astype(jnp.bfloat16)
    rest = factor - high.astype(jnp.float32)
    middle = rest.astype(jnp.bfloat16)
    low = (rest - middle.astype(jnp.float32)).astype(jnp.bfloat16)
    mix_ref[...] = jnp.concatenate([high, middle, low], axis=1)
    copies[2].wait()


def prepare(assign, probs, slab, masks, cap, after):
    toks = assign.shape[0]
    return pl.pallas_call(
        functools.partial(prepare_kernel, masks, cap),
        out_shape=[
            jax.ShapeDtypeStruct((toks, 3 * len(masks) * cap), jnp.bfloat16),
            jax.ShapeDtypeStruct(slab.shape, slab.dtype),
        ],
        in_specs=[MAIN] * 3 + [ANYWHERE],
        out_specs=[WHOLE] * 2,
        scratch_shapes=[
            pltpu.VMEM(assign.shape[::-1], assign.dtype),
            pltpu.VMEM(probs.shape[::-1], probs.dtype),
            pltpu.SemaphoreType.DMA((3,)),
        ],
        compiler_params=pltpu.CompilerParams(vmem_limit_bytes=16 * 1024 * 1024),
        cost_estimate=cost(2.5),
        name="prepare",
    )(in_main(assign.T), in_main(probs.T), in_main(slab), after)


def expert_kernel(count, steps, *refs):
    slabs, blocks, outs, rows = refs[:2], refs[2 : 2 + count], refs[2 + count : -1], refs[-1]
    units, width = slabs[0].shape[1:]
    cap = blocks[0].shape[0]
    span = width // steps
    columns = [slice(s * span, (s + 1) * span) for s in range(steps)]
    for b in range(count):
        rows[b * cap : (b + 1) * cap, :] = blocks[b][...]
    hidden = []
    for slab in slabs:
        both = jnp.zeros((2 * units, count * cap), jnp.float32)
        for c in columns:
            both = both + lax.dot_general(
                slab[0:2, :, c].reshape(2 * units, span),
                rows[:, c],
                NT,
                preferred_element_type=jnp.float32,
            )
        hidden.append((jax.nn.silu(both[:units]) * both[units:]).astype(jnp.bfloat16))
    hidden = jnp.concatenate(hidden, axis=0).T
    for c in columns:
        down = jnp.concatenate([slab[2, :, c] for slab in slabs], axis=0)
        part = jnp.dot(hidden, down, preferred_element_type=jnp.float32)
        start = 0
        for out in outs:
            stop = start + out.shape[0]
            out[:, c] = part[start:stop].astype(out.dtype)
            start = stop


def expert_part(own, sibling, blocks, wanted, steps=8):
    keys = [key for some, _ in wanted for key in some]
    cap, width = blocks[keys[0]].shape
    shapes = [jax.ShapeDtypeStruct((len(some) * cap, width), kind) for some, kind in wanted]
    return pl.pallas_call(
        functools.partial(expert_kernel, len(keys), steps),
        out_shape=shapes,
        in_specs=[WHOLE] * (2 + len(keys)),
        out_specs=[WHOLE] * len(shapes),
        scratch_shapes=[pltpu.VMEM((len(keys) * cap, width), jnp.bfloat16)],
        compiler_params=pltpu.CompilerParams(
            vmem_limit_bytes=(12 + len(keys)) * 1024 * 1024
        ),
        cost_estimate=cost(2.5),
        name="experts",
    )(own, sibling, *[blocks[k] for k in keys])


def combine_kernel(count, near, chips, steps, mix_ref, *refs):
    blocks, home, pairs = refs[:count], refs[count], refs[count + 1 : count + 1 + near]
    gots, (out_ref, held, sems) = refs[count + 1 + near : -3], refs[-3:]
    span = held.shape[1] // steps
    copies = []
    for s in range(steps):
        c = slice(s * span, (s + 1) * span)
        homes = [home[:, c]] + [pair[:, c].astype(jnp.float32) for pair in pairs]
        homes = jnp.concatenate(homes, axis=0)
        for n in range(chips - 1):
            group = gots[n * (near + 1) : (n + 1) * (near + 1)]
            homes = homes + jnp.concatenate([got[:, c] for got in group], axis=0).astype(jnp.float32)
        rows = jnp.concatenate([ref[:, c] for ref in blocks] + [homes.astype(jnp.bfloat16)], axis=0)
        held[:, c] = jnp.dot(
            mix_ref[...], jnp.concatenate([rows] * 3, axis=0), preferred_element_type=jnp.float32
        ).astype(jnp.bfloat16)
        copies.append(pltpu.make_async_copy(held.at[:, c], out_ref.at[:, c], sems.at[s]))
        copies[-1].start()
    for copy in copies:
        copy.wait()


def combine(mix, returned, home, pairs, gots, steps=4):
    count, near, chips = len(returned), len(pairs), lax.axis_size("expert") // 2
    width = home.shape[1]
    toks = mix.shape[0]
    arrays = [mix, *returned, home, *pairs, *gots]
    return pl.pallas_call(
        functools.partial(combine_kernel, count, near, chips, steps),
        out_shape=jax.ShapeDtypeStruct((toks, width), jnp.bfloat16),
        in_specs=[WHOLE] * len(arrays),
        out_specs=ANYWHERE,
        scratch_shapes=[
            pltpu.VMEM((toks, width), jnp.bfloat16),
            pltpu.SemaphoreType.DMA((steps,)),
        ],
        compiler_params=pltpu.CompilerParams(vmem_limit_bytes=12 * 1024 * 1024),
        cost_estimate=cost(1.2),
        name="combine",
    )(*arrays)


def after(x, *others):
    return lax.optimization_barrier((x, *others))[0]


def local(tokens, assign, probs, expert_weights):
    experts = lax.axis_size("dp")
    chips = lax.axis_size("expert") // 2
    cap = tokens.shape[0] // 8
    own = expert_weights[0]
    near, far = list(range(1, experts // 2)), list(range(experts // 2, experts))
    soon, late = far[: len(far) // 2], far[len(far) // 2 :]
    others = range(1, chips)

    leave = [*soon, *late, *near, 0]
    outgoing = dict(zip(leave, dispatch(assign, tokens, leave, cap)))
    blocks = {(0, 0): outgoing[0]}

    def across(m, *before):
        for c in others:
            blocks[m, c] = swap(after(blocks[m, 0], *before), "expert", 2 * c)

    across(0)
    for m in [*soon, *near, *late]:
        blocks[m, 0] = swap(outgoing[m], "dp", m)
    sibling = swap(after(own, outgoing[0]), "expert", 1)
    order = [*soon, *late, 0, *near]
    mix, own = prepare(assign, probs, own, order, cap, blocks[0, chips - 1])
    for m in soon:
        across(m, mix)
    for m in [*near, *late]:
        across(m)

    def share(m, home=jnp.float32):
        return {(m, c): jnp.bfloat16 if c else home for c in range(chips)}

    def compute(wanted):
        kinds = [([key], kind) for key, kind in wanted.items()]
        return dict(zip(wanted, expert_part(own, sibling, blocks, kinds)))

    wanted = {}
    for m in late:
        wanted |= share(m)
    parts = compute(wanted)
    came = {(m, c): swap(parts[m, c], "expert", 2 * c) for m in late for c in others}
    blocks[soon[0], 0] = after(blocks[soon[0], 0], parts[late[0], 0])
    wanted = {}
    for m in soon:
        wanted |= share(m)
    for m in near:
        wanted |= share(m, jnp.bfloat16)
    parts |= compute(wanted | share(0))
    first = came[late[-1], chips - 1]
    for m in soon:
        for c in others:
            came[m, c] = swap(after(parts[m, c], came[late[0], c]), "expert", 2 * c)

    pairs = [[swap(after(parts[m, c], first), "dp", m) for c in range(chips)] for m in near]
    returned = {}
    for m in [*late, *soon]:
        row = parts[m, 0]
        for c in others:
            row = row + came[m, c].astype(jnp.float32)
        returned[m] = swap(row.astype(jnp.bfloat16), "dp", m)
    homes = {c: swap(after(parts[0, c], first), "expert", 2 * c) for c in others}
    gots = []
    for c in others:
        gots += [homes[c]] + [swap(pair[c], "expert", 2 * c) for pair in pairs]
    return combine(
        mix, [returned[m] for m in [*soon, *late]], parts[0, 0], [pair[0] for pair in pairs], gots
    )


def solution(mesh):
    placed = (
        P(("groups", "dp", "expert"), None),
        P(("groups", "dp", "expert"), None),
        P(("groups", "dp", "expert"), None),
        P("dp", None, "expert", None),
    )
    return jax.shard_map(
        local,
        mesh=mesh,
        in_specs=placed,
        out_specs=P(("groups", "dp", "expert"), None),
        check_vma=False,
    )
```

```python
import functools
import jax
import jax.numpy as jnp
from jax import lax
from jax.experimental import pallas as pl
from jax.experimental.pallas import tpu as pltpu
from jax.sharding import PartitionSpec as P

NT = (((1,), (1,)), ((), ()))
WHOLE = pl.BlockSpec(memory_space=pltpu.VMEM)
ANYWHERE = pl.BlockSpec(memory_space=pl.ANY)
MAIN = pl.BlockSpec(memory_space=pltpu.HBM)


def swap(block, axis, mask):
    route = [(i ^ mask, i) for i in range(lax.axis_size(axis))]
    return lax.ppermute(block, axis, route)


def cost(micros):
    return pl.CostEstimate(flops=0, bytes_accessed=int(micros * 3690e3 * 1), transcendentals=0)


def in_main(x):
    return pltpu.with_memory_space_constraint(x, pltpu.HBM)


def slot_table(labels, cap, assign, probs):
    top, toks = assign.shape
    slots = len(labels) * cap
    place = lax.broadcasted_iota(jnp.int32, (slots, toks), 0)
    label = jnp.zeros((slots, toks), jnp.int32)
    for n, expert in enumerate(labels):
        label = jnp.where(place // cap == n, expert, label)
    hit = jnp.zeros((slots, toks), jnp.float32)
    weight = jnp.zeros((slots, toks), jnp.float32)
    for k in range(top):
        same = assign[k : k + 1, :] == label
        hit = jnp.where(same, 1.0, hit)
        if probs is not None:
            weight = jnp.where(same, probs[k : k + 1, :], weight)
    first = lax.broadcasted_iota(jnp.int32, (toks, toks), 0)
    second = lax.broadcasted_iota(jnp.int32, (toks, toks), 1)
    position = jnp.dot(
        hit.astype(jnp.bfloat16),
        (first < second).astype(jnp.bfloat16),
        preferred_element_type=jnp.float32,
    )
    here = (hit > 0.0) & (position == (place % cap).astype(jnp.float32))
    return here, weight


def dispatch_kernel(masks, cap, steps, assign_ref, tok_ref, *refs):
    outs, (table, held, sems) = refs[: len(masks)], refs[len(masks) :]
    span = held.shape[1] // steps
    columns = [slice(s * span, (s + 1) * span) for s in range(steps)]
    small = pltpu.make_async_copy(assign_ref, table, sems.at[steps])
    small.start()
    copies = [
        pltpu.make_async_copy(tok_ref.at[:, c], held.at[:, c], sems.at[s])
        for s, c in enumerate(columns)
    ]
    for copy in copies:
        copy.start()
    small.wait()
    me = lax.axis_index("dp")
    here, _ = slot_table([me ^ m for m in masks], cap, table[...], None)
    pick = here.astype(jnp.bfloat16)
    for copy, c in zip(copies, columns):
        copy.wait()
        rows = jnp.dot(pick, held[:, c], preferred_element_type=jnp.float32)
        rows = rows.astype(jnp.bfloat16)
        for n in range(len(masks)):
            outs[n][:, c] = rows[n * cap : (n + 1) * cap]


def dispatch(assign, tokens, masks, cap, steps=2):
    toks, width = tokens.shape
    return pl.pallas_call(
        functools.partial(dispatch_kernel, masks, cap, steps),
        out_shape=[jax.ShapeDtypeStruct((cap, width), jnp.bfloat16)] * len(masks),
        in_specs=[MAIN, MAIN],
        out_specs=[WHOLE] * len(masks),
        scratch_shapes=[
            pltpu.VMEM(assign.shape[::-1], assign.dtype),
            pltpu.VMEM((toks, width), jnp.bfloat16),
            pltpu.SemaphoreType.DMA((steps + 1,)),
        ],
        compiler_params=pltpu.CompilerParams(vmem_limit_bytes=12 * 1024 * 1024),
        cost_estimate=cost(1.0),
        name="dispatch",
    )(in_main(assign.T), in_main(tokens))


def prepare_kernel(
    masks, cap, assign_ref, probs_ref, slab_ref, after_ref, mix_ref, held_ref, ids, gains, sems
):
    copies = [
        pltpu.make_async_copy(assign_ref, ids, sems.at[0]),
        pltpu.make_async_copy(probs_ref, gains, sems.at[1]),
        pltpu.make_async_copy(slab_ref, held_ref, sems.at[2]),
    ]
    for copy in copies:
        copy.start()
    copies[0].wait()
    copies[1].wait()
    me = lax.axis_index("dp")
    here, weight = slot_table([me ^ m for m in masks], cap, ids[...], gains[...])
    factor = jnp.where(here, weight, 0.0).T
    high = factor.astype(jnp.bfloat16)
    rest = factor - high.astype(jnp.float32)
    middle = rest.astype(jnp.bfloat16)
    low = (rest - middle.astype(jnp.float32)).astype(jnp.bfloat16)
    mix_ref[...] = jnp.concatenate([high, middle, low], axis=1)
    copies[2].wait()


def prepare(assign, probs, slab, masks, cap, after):
    toks = assign.shape[0]
    return pl.pallas_call(
        functools.partial(prepare_kernel, masks, cap),
        out_shape=[
            jax.ShapeDtypeStruct((toks, 3 * len(masks) * cap), jnp.bfloat16),
            jax.ShapeDtypeStruct(slab.shape, slab.dtype),
        ],
        in_specs=[MAIN] * 3 + [ANYWHERE],
        out_specs=[WHOLE] * 2,
        scratch_shapes=[
            pltpu.VMEM(assign.shape[::-1], assign.dtype),
            pltpu.VMEM(probs.shape[::-1], probs.dtype),
            pltpu.SemaphoreType.DMA((3,)),
        ],
        compiler_params=pltpu.CompilerParams(vmem_limit_bytes=16 * 1024 * 1024),
        cost_estimate=cost(2.5),
        name="prepare",
    )(in_main(assign.T), in_main(probs.T), in_main(slab), after)


def expert_kernel(count, steps, *refs):
    slabs, blocks, outs, rows = refs[:2], refs[2 : 2 + count], refs[2 + count : -1], refs[-1]
    units, width = slabs[0].shape[1:]
    cap = blocks[0].shape[0]
    span = width // steps
    columns = [slice(s * span, (s + 1) * span) for s in range(steps)]
    for b in range(count):
        rows[b * cap : (b + 1) * cap, :] = blocks[b][...]
    hidden = []
    for slab in slabs:
        both = jnp.zeros((2 * units, count * cap), jnp.float32)
        for c in columns:
            both = both + lax.dot_general(
                slab[0:2, :, c].reshape(2 * units, span),
                rows[:, c],
                NT,
                preferred_element_type=jnp.float32,
            )
        hidden.append((jax.nn.silu(both[:units]) * both[units:]).astype(jnp.bfloat16))
    hidden = jnp.concatenate(hidden, axis=0).T
    for c in columns:
        down = jnp.concatenate([slab[2, :, c] for slab in slabs], axis=0)
        part = jnp.dot(hidden, down, preferred_element_type=jnp.float32)
        start = 0
        for out in outs:
            stop = start + out.shape[0]
            out[:, c] = part[start:stop].astype(out.dtype)
            start = stop


def expert_part(own, sibling, blocks, wanted, steps=8):
    keys = [key for some, _ in wanted for key in some]
    cap, width = blocks[keys[0]].shape
    shapes = [jax.ShapeDtypeStruct((len(some) * cap, width), kind) for some, kind in wanted]
    return pl.pallas_call(
        functools.partial(expert_kernel, len(keys), steps),
        out_shape=shapes,
        in_specs=[WHOLE] * (2 + len(keys)),
        out_specs=[WHOLE] * len(shapes),
        scratch_shapes=[pltpu.VMEM((len(keys) * cap, width), jnp.bfloat16)],
        compiler_params=pltpu.CompilerParams(
            vmem_limit_bytes=(12 + len(keys)) * 1024 * 1024
        ),
        cost_estimate=cost(2.5),
        name="experts",
    )(own, sibling, *[blocks[k] for k in keys])


def combine_kernel(count, near, chips, steps, mix_ref, *refs):
    blocks, home, pairs = refs[:count], refs[count], refs[count + 1 : count + 1 + near]
    gots, (out_ref, held, sems) = refs[count + 1 + near : -3], refs[-3:]
    cap = home.shape[0]
    span = held.shape[1] // steps
    copies = []
    for s in range(steps):
        c = slice(s * span, (s + 1) * span)
        homes = [home[:, c]] + [pair[:cap, c].astype(jnp.float32) for pair in pairs]
        homes = jnp.concatenate(homes, axis=0)
        each = len(gots) // (chips - 1)
        for n in range(chips - 1):
            group = gots[n * each : (n + 1) * each]
            share = jnp.concatenate([got[:, c] for got in group], axis=0).astype(jnp.float32)
            if each == 1 and near:
                homes = jnp.concatenate([homes[:cap] + share, homes[cap:]], axis=0)
            else:
                homes = homes + share
        rows = jnp.concatenate([ref[:, c] for ref in blocks] + [homes.astype(jnp.bfloat16)], axis=0)
        held[:, c] = jnp.dot(
            mix_ref[...], jnp.concatenate([rows] * 3, axis=0), preferred_element_type=jnp.float32
        ).astype(jnp.bfloat16)
        copies.append(pltpu.make_async_copy(held.at[:, c], out_ref.at[:, c], sems.at[s]))
        copies[-1].start()
    for copy in copies:
        copy.wait()


def combine(mix, returned, home, pairs, gots, steps=4):
    count, near, chips = len(returned), len(pairs), lax.axis_size("expert") // 2
    width = home.shape[1]
    toks = mix.shape[0]
    arrays = [mix, *returned, home, *pairs, *gots]
    return pl.pallas_call(
        functools.partial(combine_kernel, count, near, chips, steps),
        out_shape=jax.ShapeDtypeStruct((toks, width), jnp.bfloat16),
        in_specs=[WHOLE] * len(arrays),
        out_specs=ANYWHERE,
        scratch_shapes=[
            pltpu.VMEM((toks, width), jnp.bfloat16),
            pltpu.SemaphoreType.DMA((steps,)),
        ],
        compiler_params=pltpu.CompilerParams(vmem_limit_bytes=12 * 1024 * 1024),
        cost_estimate=cost(1.2),
        name="combine",
    )(*arrays)


def after(x, *others):
    return lax.optimization_barrier((x, *others))[0]


OPT = {'co': '23', 'do': '2310', 'zo': '2130', 'sib': 'a', 'pre': 'x', 'xo': '213', 'xd1': '', 'xd2': 'm', 'xd3': '', 'bo': '23', 'back': 'x', 'od': '2n', 'nd': '3', 'pz': '1', 'A': '3', 'ab': '1', 'fd': '', 'nb': '', 'ps': '1', 'pd': '3', 'b': 'g', 'sb': '13'}


def local(tokens, assign, probs, expert_weights):
    experts = lax.axis_size("dp")
    chips = lax.axis_size("expert") // 2
    cap = tokens.shape[0] // 8
    own = expert_weights[0]
    near, far = list(range(1, experts // 2)), list(range(experts // 2, experts))
    soon, late = far[: len(far) // 2], far[len(far) // 2 :]
    lists = {"1": near, "2": soon, "3": late, "0": [0]}
    others = range(1, chips)
    blocks, came = {}, {}

    def run(code):
        return [m for k in code for m in lists[k]]

    order = run(OPT["co"]) + [0] + near
    rows_order = run(OPT["do"])
    outgoing = dict(zip(rows_order, dispatch(assign, tokens, rows_order, cap, steps=2)))
    blocks[0, 0] = outgoing[0]
    state = {}

    def dep(code):
        out = []
        for k in code:
            if k == "m":
                out.append(state["mix"])
            elif k == "x":
                out.append(blocks[0, chips - 1])
            elif k in "123":
                out.append(blocks[lists[k][-1], 0])
        return out

    for m in run(OPT["zo"]):
        if m:
            blocks[m, 0] = swap(after(outgoing[m]) if "z" in OPT["b"] else outgoing[m], "dp", m)
        else:
            for c in others:
                blocks[0, c] = swap(after(outgoing[0]) if "o" in OPT["b"] else outgoing[0], "expert", 2 * c)
    sibling = swap(own if OPT["sib"] == "s" else after(own, outgoing[0]), "expert", 1)
    pre = {"o": outgoing[0], "x": blocks[0, chips - 1], "1": blocks[near[0], 0], "3": blocks[late[0], 0]}[OPT["pre"]]
    state["mix"], held = prepare(assign, probs, after(own) if "w" in OPT["b"] else own, order, cap, pre)
    away = run(OPT["bo"])
    zfirst = OPT["back"] == "z"
    tagged = {("f", m, c): ([(m, c)], jnp.bfloat16 if c else jnp.float32) for m in away for c in range(chips)}
    for m in near:
        if zfirst and OPT["ps"]:
            tagged |= {("n", m, c): ([(m, c)], jnp.bfloat16) for c in range(chips)}
        elif zfirst:
            tagged["n", m, 0] = ([(m, c) for c in range(chips)], jnp.bfloat16)
        else:
            tagged |= {("n", m, c): ([(m, c)], jnp.bfloat16 if c else jnp.float32) for c in range(chips)}
    tagged |= {("h", 0, c): ([(0, c)], jnp.bfloat16 if c else jnp.float32) for c in range(chips)}
    early = run(OPT["A"])
    first = [t for t in tagged if t[1] in early]
    second = [t for t in tagged if t[1] not in early]
    made = {}

    def compute_first():
        made.update(zip(first, expert_part(held, sibling, blocks, [tagged[t] for t in first])))

    for code in OPT["xo"]:
        before = dep(OPT["xd" + code])
        if "a" in OPT["xd" + code]:
            compute_first()
            before.append(made[first[0]])
        for m in lists[code]:
            for c in others:
                here = after(blocks[m, 0], *before) if before or code in OPT["sb"] else blocks[m, 0]
                blocks[m, c] = swap(here, "expert", 2 * c)
    if first and not made:
        compute_first()
    if first and OPT["ab"]:
        k = tagged[second[0]][0][0]
        blocks[k] = after(blocks[k], made[first[0]])
    made |= dict(zip(second, expert_part(held, sibling, blocks, [tagged[t] for t in second])))
    for t in first:
        if t[0] in OPT["nb"]:
            made[t] = after(made[t], made[second[0]])
    pf = [made[t] for t in tagged if t[0] == "f"]
    pn = [made[t] for t in tagged if t[0] == "n"]
    ph = [made[t] for t in tagged if t[0] == "h"]
    for n, m in enumerate(away):
        for c in others:
            part = after(pf[n * chips + c]) if "p" in OPT["b"] else pf[n * chips + c]
            if OPT["fd"] and n and first and m not in early:
                part = after(part, came[away[0], c])
            came[m, c] = swap(part, "expert", 2 * c)

    def bdep(code):
        return [came[lists[k][-1], chips - 1] for k in code if k in "23"]

    returned = {}

    def send_far():
        for n, m in enumerate(away):
            row = pf[n * chips]
            for c in others:
                row = row + came[m, c].astype(jnp.float32)
            row = row.astype(jnp.bfloat16)
            if m in soon and "s" in OPT["b"] or m in late and "l" in OPT["b"]:
                row = after(row)
            returned[m] = swap(row, "dp", m)

    def send_home(*more):
        return {c: swap(after(ph[c], *bdep(OPT["od"]), *more), "expert", 2 * c) for c in others}

    if zfirst:
        def send_pairs():
            each = chips if OPT["ps"] else 1
            sent = [swap(after(part, *bdep(OPT["pd"])), "dp", near[n // each]) for n, part in enumerate(pn)]
            if OPT["ps"]:
                return [sent[n * chips : (n + 1) * chips] for n in range(len(near))]
            return [[pair[c * cap : (c + 1) * cap] for c in range(chips)] for pair in sent]

        if OPT["pz"] == "0":
            pairs = send_pairs()
            send_far()
        else:
            send_far()
            pairs = send_pairs()
        hx = send_home()
        gots = []
        for c in others:
            gots.append(hx[c])
            gots += [
                swap(after(pair[c], *bdep(OPT["nd"])) if "g" in OPT["b"] or OPT["nd"] else pair[c], "expert", 2 * c)
                for pair in pairs
            ]
        return combine(
            state["mix"], [returned[m] for m in order[: len(far)]], ph[0], [pair[0] for pair in pairs], gots
        )
    nx = {
        (m, c): swap(after(pn[n * chips + c], *bdep(OPT["nd"])), "expert", 2 * c)
        for n, m in enumerate(near)
        for c in others
    }
    send_far()
    hx = send_home(*([nx[near[-1], chips - 1]] if "n" in OPT["od"] else []))
    for n, m in enumerate(near):
        row = pn[n * chips]
        for c in others:
            row = row + nx[m, c].astype(jnp.float32)
        returned[m] = swap(row.astype(jnp.bfloat16), "dp", m)
    gots = [hx[c] for c in others]
    return combine(state["mix"], [returned[m] for m in order[: len(far)]], ph[0], [returned[m] for m in near], gots)


def solution(mesh):
    placed = (
        P(("groups", "dp", "expert"), None),
        P(("groups", "dp", "expert"), None),
        P(("groups", "dp", "expert"), None),
        P("dp", None, "expert", None),
    )
    return jax.shard_map(
        local,
        mesh=mesh,
        in_specs=placed,
        out_specs=P(("groups", "dp", "expert"), None),
        check_vma=False,
    )
```

```python
import functools
import jax
import jax.numpy as jnp
from jax import lax
from jax.experimental import pallas as pl
from jax.experimental.pallas import tpu as pltpu
from jax.sharding import PartitionSpec as P

NT = (((1,), (1,)), ((), ()))
WHOLE = pl.BlockSpec(memory_space=pltpu.VMEM)
ANYWHERE = pl.BlockSpec(memory_space=pl.ANY)
MAIN = pl.BlockSpec(memory_space=pltpu.HBM)


def swap(block, axis, mask):
    route = [(i ^ mask, i) for i in range(lax.axis_size(axis))]
    return lax.ppermute(block, axis, route)


def cost(micros):
    return pl.CostEstimate(flops=0, bytes_accessed=int(micros * 3690e3), transcendentals=0)


def in_main(x):
    return pltpu.with_memory_space_constraint(x, pltpu.HBM)


def slot_table(labels, cap, assign, probs):
    top, toks = assign.shape
    slots = len(labels) * cap
    place = lax.broadcasted_iota(jnp.int32, (slots, toks), 0)
    label = jnp.zeros((slots, toks), jnp.int32)
    for n, expert in enumerate(labels):
        label = jnp.where(place // cap == n, expert, label)
    hit = jnp.zeros((slots, toks), jnp.float32)
    weight = jnp.zeros((slots, toks), jnp.float32)
    for k in range(top):
        same = assign[k : k + 1, :] == label
        hit = jnp.where(same, 1.0, hit)
        if probs is not None:
            weight = jnp.where(same, probs[k : k + 1, :], weight)
    first = lax.broadcasted_iota(jnp.int32, (toks, toks), 0)
    second = lax.broadcasted_iota(jnp.int32, (toks, toks), 1)
    position = jnp.dot(
        hit.astype(jnp.bfloat16),
        (first < second).astype(jnp.bfloat16),
        preferred_element_type=jnp.float32,
    )
    here = (hit > 0.0) & (position == (place % cap).astype(jnp.float32))
    return here, weight


def dispatch_kernel(masks, cap, steps, assign_ref, tok_ref, *refs):
    outs, (table, held, sems) = refs[: len(masks)], refs[len(masks) :]
    span = held.shape[1] // steps
    columns = [slice(s * span, (s + 1) * span) for s in range(steps)]
    small = pltpu.make_async_copy(assign_ref, table, sems.at[steps])
    small.start()
    copies = [
        pltpu.make_async_copy(tok_ref.at[:, c], held.at[:, c], sems.at[s])
        for s, c in enumerate(columns)
    ]
    for copy in copies:
        copy.start()
    small.wait()
    me = lax.axis_index("dp")
    here, _ = slot_table([me ^ m for m in masks], cap, table[...], None)
    pick = here.astype(jnp.bfloat16)
    for copy, c in zip(copies, columns):
        copy.wait()
        rows = jnp.dot(pick, held[:, c], preferred_element_type=jnp.float32)
        rows = rows.astype(jnp.bfloat16)
        for n in range(len(masks)):
            outs[n][:, c] = rows[n * cap : (n + 1) * cap]


def dispatch(assign, tokens, masks, cap, steps=2):
    toks, width = tokens.shape
    return pl.pallas_call(
        functools.partial(dispatch_kernel, masks, cap, steps),
        out_shape=[jax.ShapeDtypeStruct((cap, width), jnp.bfloat16)] * len(masks),
        in_specs=[MAIN, MAIN],
        out_specs=[WHOLE] * len(masks),
        scratch_shapes=[
            pltpu.VMEM(assign.shape[::-1], assign.dtype),
            pltpu.VMEM((toks, width), jnp.bfloat16),
            pltpu.SemaphoreType.DMA((steps + 1,)),
        ],
        compiler_params=pltpu.CompilerParams(vmem_limit_bytes=12 * 1024 * 1024),
        cost_estimate=cost(1.0),
        name="dispatch",
    )(in_main(assign.T), in_main(tokens))


def prepare_kernel(
    masks, cap, assign_ref, probs_ref, slab_ref, after_ref, mix_ref, held_ref, ids, gains, sems
):
    copies = [
        pltpu.make_async_copy(assign_ref, ids, sems.at[0]),
        pltpu.make_async_copy(probs_ref, gains, sems.at[1]),
        pltpu.make_async_copy(slab_ref, held_ref, sems.at[2]),
    ]
    for copy in copies:
        copy.start()
    copies[0].wait()
    copies[1].wait()
    me = lax.axis_index("dp")
    here, weight = slot_table([me ^ m for m in masks], cap, ids[...], gains[...])
    factor = jnp.where(here, weight, 0.0).T
    high = factor.astype(jnp.bfloat16)
    rest = factor - high.astype(jnp.float32)
    middle = rest.astype(jnp.bfloat16)
    low = (rest - middle.astype(jnp.float32)).astype(jnp.bfloat16)
    mix_ref[...] = jnp.concatenate([high, middle, low], axis=1)
    copies[2].wait()


def prepare(assign, probs, slab, masks, cap, after):
    toks = assign.shape[0]
    return pl.pallas_call(
        functools.partial(prepare_kernel, masks, cap),
        out_shape=[
            jax.ShapeDtypeStruct((toks, 3 * len(masks) * cap), jnp.bfloat16),
            jax.ShapeDtypeStruct(slab.shape, slab.dtype),
        ],
        in_specs=[MAIN] * 3 + [ANYWHERE],
        out_specs=[WHOLE] * 2,
        scratch_shapes=[
            pltpu.VMEM(assign.shape[::-1], assign.dtype),
            pltpu.VMEM(probs.shape[::-1], probs.dtype),
            pltpu.SemaphoreType.DMA((3,)),
        ],
        compiler_params=pltpu.CompilerParams(vmem_limit_bytes=16 * 1024 * 1024),
        cost_estimate=cost(2.5),
        name="prepare",
    )(in_main(assign.T), in_main(probs.T), in_main(slab), after)


def expert_kernel(count, steps, *refs):
    slabs, blocks, outs, rows = refs[:2], refs[2 : 2 + count], refs[2 + count : -1], refs[-1]
    units, width = slabs[0].shape[1:]
    cap = blocks[0].shape[0]
    span = width // steps
    columns = [slice(s * span, (s + 1) * span) for s in range(steps)]
    for b in range(count):
        rows[b * cap : (b + 1) * cap, :] = blocks[b][...]
    hidden = []
    for slab in slabs:
        both = jnp.zeros((2 * units, count * cap), jnp.float32)
        for c in columns:
            both = both + lax.dot_general(
                slab[0:2, :, c].reshape(2 * units, span),
                rows[:, c],
                NT,
                preferred_element_type=jnp.float32,
            )
        hidden.append((jax.nn.silu(both[:units]) * both[units:]).astype(jnp.bfloat16))
    hidden = jnp.concatenate(hidden, axis=0).T
    for c in columns:
        down = jnp.concatenate([slab[2, :, c] for slab in slabs], axis=0)
        part = jnp.dot(hidden, down, preferred_element_type=jnp.float32)
        start = 0
        for out in outs:
            stop = start + out.shape[0]
            out[:, c] = part[start:stop].astype(out.dtype)
            start = stop


def expert_part(own, sibling, blocks, wanted, steps=8):
    keys = [key for some, _ in wanted for key in some]
    cap, width = blocks[keys[0]].shape
    shapes = [jax.ShapeDtypeStruct((len(some) * cap, width), kind) for some, kind in wanted]
    return pl.pallas_call(
        functools.partial(expert_kernel, len(keys), steps),
        out_shape=shapes,
        in_specs=[WHOLE] * (2 + len(keys)),
        out_specs=[WHOLE] * len(shapes),
        scratch_shapes=[pltpu.VMEM((len(keys) * cap, width), jnp.bfloat16)],
        compiler_params=pltpu.CompilerParams(
            vmem_limit_bytes=(12 + len(keys)) * 1024 * 1024
        ),
        cost_estimate=cost(2.5),
        name="experts",
    )(own, sibling, *[blocks[k] for k in keys])


def combine_kernel(count, near, chips, steps, mix_ref, *refs):
    blocks, home, pairs = refs[:count], refs[count], refs[count + 1 : count + 1 + near]
    gots, (out_ref, held, sems) = refs[count + 1 + near : -3], refs[-3:]
    span = held.shape[1] // steps
    copies = []
    for s in range(steps):
        c = slice(s * span, (s + 1) * span)
        homes = [home[:, c]] + [pair[:, c].astype(jnp.float32) for pair in pairs]
        homes = jnp.concatenate(homes, axis=0)
        for n in range(chips - 1):
            group = gots[n * (near + 1) : (n + 1) * (near + 1)]
            homes = homes + jnp.concatenate([got[:, c] for got in group], axis=0).astype(jnp.float32)
        rows = jnp.concatenate([ref[:, c] for ref in blocks] + [homes.astype(jnp.bfloat16)], axis=0)
        held[:, c] = jnp.dot(
            mix_ref[...], jnp.concatenate([rows] * 3, axis=0), preferred_element_type=jnp.float32
        ).astype(jnp.bfloat16)
        copies.append(pltpu.make_async_copy(held.at[:, c], out_ref.at[:, c], sems.at[s]))
        copies[-1].start()
    for copy in copies:
        copy.wait()


def combine(mix, returned, home, pairs, gots, steps=4):
    count, near, chips = len(returned), len(pairs), lax.axis_size("expert") // 2
    width = home.shape[1]
    toks = mix.shape[0]
    arrays = [mix, *returned, home, *pairs, *gots]
    return pl.pallas_call(
        functools.partial(combine_kernel, count, near, chips, steps),
        out_shape=jax.ShapeDtypeStruct((toks, width), jnp.bfloat16),
        in_specs=[WHOLE] * len(arrays),
        out_specs=ANYWHERE,
        scratch_shapes=[
            pltpu.VMEM((toks, width), jnp.bfloat16),
            pltpu.SemaphoreType.DMA((steps,)),
        ],
        compiler_params=pltpu.CompilerParams(vmem_limit_bytes=12 * 1024 * 1024),
        cost_estimate=cost(1.2),
        name="combine",
    )(*arrays)


def after(x, *others):
    return lax.optimization_barrier((x, *others))[0]


def local(tokens, assign, probs, expert_weights):
    experts = lax.axis_size("dp")
    chips = lax.axis_size("expert") // 2
    cap = tokens.shape[0] // 8
    own = expert_weights[0]
    near, far = list(range(1, experts // 2)), list(range(experts // 2, experts))
    soon, late = far[: len(far) // 2], far[len(far) // 2 :]
    others = range(1, chips)

    leave = [*soon, *late, *near, 0]
    outgoing = dict(zip(leave, dispatch(assign, tokens, leave, cap)))
    blocks = {(0, 0): outgoing[0]}

    def across(m, *before):
        for c in others:
            blocks[m, c] = swap(after(blocks[m, 0], *before), "expert", 2 * c)

    across(0)
    for m in [*soon, *near, *late]:
        blocks[m, 0] = swap(outgoing[m], "dp", m)
    sibling = swap(own, "expert", 1)
    order = [*soon, *late, 0, *near]
    mix, own = prepare(assign, probs, own, order, cap, blocks[0, chips - 1])
    for m in soon:
        across(m, mix)
    for m in [*near, *late]:
        across(m)

    def share(m, home=jnp.float32):
        return {(m, c): jnp.bfloat16 if c else home for c in range(chips)}

    def compute(wanted):
        kinds = [([key], kind) for key, kind in wanted.items()]
        return dict(zip(wanted, expert_part(own, sibling, blocks, kinds)))

    wanted = {}
    for m in late:
        wanted |= share(m)
    parts = compute(wanted)
    came = {(m, c): swap(parts[m, c], "expert", 2 * c) for m in late for c in others}
    blocks[soon[0], 0] = after(blocks[soon[0], 0], parts[late[0], 0])
    wanted = {}
    for m in soon:
        wanted |= share(m)
    for m in near:
        wanted |= share(m, jnp.bfloat16)
    parts |= compute(wanted | share(0))
    first = came[late[-1], chips - 1]
    for m in soon:
        for c in others:
            came[m, c] = swap(after(parts[m, c], came[late[0], c]), "expert", 2 * c)

    pairs = [[swap(after(parts[m, c], first), "dp", m) for c in range(chips)] for m in near]
    returned = {}
    for m in [*late, *soon]:
        row = parts[m, 0]
        for c in others:
            row = row + came[m, c].astype(jnp.float32)
        returned[m] = swap(row.astype(jnp.bfloat16), "dp", m)
    homes = {c: swap(after(parts[0, c], first), "expert", 2 * c) for c in others}
    gots = []
    for c in others:
        gots += [homes[c]] + [swap(pair[c], "expert", 2 * c) for pair in pairs]
    return combine(
        mix, [returned[m] for m in [*soon, *late]], parts[0, 0], [pair[0] for pair in pairs], gots
    )


def solution(mesh):
    placed = (
        P(("groups", "dp", "expert"), None),
        P(("groups", "dp", "expert"), None),
        P(("groups", "dp", "expert"), None),
        P("dp", None, "expert", None),
    )
    return jax.shard_map(
        local,
        mesh=mesh,
        in_specs=placed,
        out_specs=P(("groups", "dp", "expert"), None),
        check_vma=False,
    )
```
